32 devices in a mesh: grp: 2 (over x), uly: 8 (over z, y), blk: 2 (over core).
Axes of the slice: x: 2, y: 2, z: 4, core: 2. Of those that a mesh axis runs over, the one named last changes fastest.
Arguments:
- queries: bfloat16 [8192, 8, 128], P(('grp', 'uly', 'blk')), parts along dimension 0, may hold values from -8 to 8
- keys: bfloat16 [8192, 8, 128], P(('grp', 'uly', 'blk')), parts along dimension 0, may hold values from -8 to 8
- values: bfloat16 [8192, 8, 128], P(('grp', 'uly', 'blk')), parts along dimension 0, may hold values from -6 to 6
- pattern: int32 [16, 32, 8], P(('grp', 'uly')), parts along dimension 0, may hold values from 0 to 31, as said below
- heavy: int32 [16, 2], P(('grp', 'uly')), parts along dimension 0, may hold values from 0 to 31, as said below
Outputs:
- attended: bfloat16 [8192, 8, 128], P(('grp', 'uly', 'blk')), parts along dimension 0
The draws below stay inside these ranges and needn't reach their ends.
There are 2 independent parts, one for each index of `grp`. The reference program is written for one: setup_inputs(seed, part) draws one part's arguments, and reference() takes and returns one part's arrays. A program takes and returns all parts, laid end to end along the dimension named above; each array names one. Nothing has to cross between parts.
Inputs may be any that keep to these rules, and one draw needn't show every extreme that they name: `pattern`: row t of each head lists 8 distinct tiles, the first of them t itself. `heavy`: each head lists 2 distinct tiles.
All inputs are finite; a program needn't handle non-finite values.
Results may differ from the reference program's by a relative error of at most 0.0075.
Values may be sent and summed in bfloat16 or wider, within the bound.
A program may use at most 64 MiB of HBM per device.

```python
import jax
import jax.numpy as jnp
from jax import lax

HD = 128
TILE = 128
KT = 8
HEAVY = 2
TOK_DEV = 256
HEADS = 8
SEQ = 4096
TILES = 32


def draw_queries(key, part):
    key = jax.random.fold_in(key, 11)
    spread = jnp.clip(jax.random.normal(key, (TILES, TILE, HEADS, HD), jnp.float32), -6.0, 6.0)
    return spread.reshape(SEQ, HEADS, HD).astype(jnp.bfloat16)


def draw_keys(key, part):
    key = jax.random.fold_in(key, 13)
    spread = jnp.clip(jax.random.normal(key, (TILES, TILE, HEADS, HD), jnp.float32), -6.0, 6.0)
    return spread.reshape(SEQ, HEADS, HD).astype(jnp.bfloat16)


def draw_pattern(key, part):
    key = jax.random.fold_in(key, 23)
    ident = jnp.arange(TILES, dtype=jnp.int32)
    scores = jax.random.randint(key, (HEADS, TILES, TILES), 0, 2 ** 16) * TILES + ident[None, None, :]
    scores = jnp.where((ident[:, None] == ident[None, :])[None], 2 ** 30, scores)
    return lax.top_k(scores, KT)[1].astype(jnp.int32)


def draw_heavy(key, part):
    key = jax.random.fold_in(key, 37)
    noise_key, count_key, lean_key = jax.random.split(key, 3)
    ident = jnp.arange(TILES, dtype=jnp.int32)
    scores = jax.random.randint(noise_key, (HEADS, TILES), 0, 2 ** 16) * TILES + ident[None, :]
    parity = ident // (TOK_DEV // TILE) % 2
    first = lax.top_k(jnp.where(parity[None, :] == 0, scores, -1), HEAVY)[1]
    second = lax.top_k(jnp.where(parity[None, :] == 1, scores, -1), HEAVY)[1]
    counts = jax.random.randint(count_key, (HEADS,), 0, HEAVY + 1)
    leaning = jax.random.randint(lean_key, (), 0, 2) * HEAVY
    counts = counts.at[0].set(leaning)
    column = jnp.arange(HEAVY, dtype=jnp.int32)[None, :]
    later = jnp.take_along_axis(second, jnp.clip(column - counts[:, None], 0, HEAVY - 1), axis=1)
    return jnp.where(column < counts[:, None], first, later).astype(jnp.int32)


def level_of(own_key, shape, pieces, smallest, top_value):
    gain, own = 1.0, jax.random.fold_in(own_key, 6)
    for position, parts in pieces:
        draws = jnp.exp(jax.random.uniform(jax.random.fold_in(own, position), (parts,), jnp.float32, smallest / len(pieces), top_value / len(pieces)))
        gain = gain * jnp.repeat(draws, shape[position] // parts).reshape([-1 if axis == position else 1 for axis in range(len(shape))])
    return gain


def normal_values(own_key, extent, scale, bound, pieces=(), kind=jnp.bfloat16):
    level = level_of(own_key, extent, pieces, -0.22, 0.18) if pieces else 1.0
    entries = jax.random.normal(own_key, extent, jnp.float32) * scale * level
    return jnp.minimum(jnp.maximum(entries, -bound), bound).astype(kind)


def setup_inputs(seed: int = 0, part: int = 0) -> dict:
    streams_of = jax.random.split(jax.random.key(seed), 6)
    part_splits = jax.random.split(jax.random.fold_in(streams_of[5], part), 6)
    return {
        "queries": draw_queries(jax.random.fold_in(jax.random.fold_in(streams_of[5], part), 71), part),
        "keys": draw_keys(jax.random.fold_in(jax.random.fold_in(streams_of[5], part), 71), part),
        "values": normal_values(part_splits[2], (SEQ, HEADS, HD), 1.0, 6.0, ((0, 16),)),
        "pattern": draw_pattern(jax.random.fold_in(jax.random.fold_in(streams_of[5], part), 71), part),
        "heavy": draw_heavy(jax.random.fold_in(jax.random.fold_in(streams_of[5], part), 71), part),
    }


def attend(query_rows, key_rows, value_rows):
    scores = jnp.einsum("gqd,gkd->gqk", query_rows.astype(jnp.float32), key_rows.astype(jnp.float32)) * (HD ** -0.5)
    row_max = jnp.max(scores, axis=-1, keepdims=True)
    weights = jnp.exp(scores - row_max)
    row_total = jnp.sum(weights, axis=-1, keepdims=True)
    probabilities = weights.astype(jnp.bfloat16)
    blended = jnp.einsum("gqk,gkd->gqd", probabilities.astype(jnp.float32), value_rows.astype(jnp.float32))
    return (blended / row_total).astype(jnp.bfloat16)


def one_head(inputs):
    query_head, key_head, value_head, pattern_head, heavy_head = inputs
    query_tiles = query_head.reshape(TILES, TILE, HD)
    key_tiles = key_head.reshape(TILES, TILE, HD)
    value_tiles = value_head.reshape(TILES, TILE, HD)
    chosen_keys = key_tiles[pattern_head].reshape(TILES, KT * TILE, HD)
    chosen_values = value_tiles[pattern_head].reshape(TILES, KT * TILE, HD)
    sparse_out = attend(query_tiles, chosen_keys, chosen_values)
    dense_queries = query_tiles[heavy_head]
    all_keys = jnp.broadcast_to(key_head[None], (HEAVY, SEQ, HD))
    all_values = jnp.broadcast_to(value_head[None], (HEAVY, SEQ, HD))
    dense_out = attend(dense_queries, all_keys, all_values)
    sparse_out = sparse_out.at[heavy_head].set(dense_out)
    return sparse_out.reshape(SEQ, HD)


def reference(queries, keys, values, pattern, heavy):
    per_head = lax.map(one_head, (jnp.moveaxis(queries, 1, 0), jnp.moveaxis(keys, 1, 0), jnp.moveaxis(values, 1, 0), pattern, heavy))
    return jnp.moveaxis(per_head, 0, 1)
```

```python
import functools
import math

import jax
import jax.numpy as jnp
from jax import lax
from jax.experimental import pallas as pl
from jax.experimental.pallas import tpu as pltpu
from jax.sharding import PartitionSpec as P

TILE = 128
MESH = pl.DeviceIdType.MESH


def flip(u, d, count):
    if count & (count - 1):
        return (d + count - u) % count
    out, k = 0, 1
    while k < count:
        out = out + ((u // k + d // k) % 2) * k
        k *= 2
    return out


def kernel(
    U, per, pat, heavy, q_in, k_in, v_in, out,
    Q, K, V, probs, total, dense_p, dense_o, o_send,
    send_sem, recv_sem, fsend_sem, frecv_sem, loc_sem, osend_sem, orecv_sem,
):
    u, b = lax.axis_index("uly"), lax.axis_index("blk")
    sib = 1 - b
    tiles, head = K.shape[0], K.shape[2]
    listed, heavies = pat.shape[2], heavy.shape[1]
    c2 = head ** (-0.5) * math.log2(math.e)
    group = math.gcd(tiles, 8)
    bufs, ins = (K, Q, V), (k_in, q_in, v_in)

    barrier = pltpu.get_barrier_semaphore()

    def greet(d, c):
        pl.semaphore_signal(
            barrier, inc=1, device_id={"uly": flip(u, d, U), "blk": b}, device_id_type=MESH
        )
        return c

    lax.fori_loop(1, U, greet, 0)
    pl.semaphore_signal(barrier, inc=1, device_id={"uly": u, "blk": sib}, device_id_type=MESH)
    pl.semaphore_wait(barrier, U)

    def at(buf, s, half):
        return buf.at[pl.ds((s * 2 + half) * per, per)]

    def away(n, s):
        return pltpu.make_async_remote_copy(
            src_ref=ins[n].at[s], dst_ref=at(bufs[n], u, b),
            send_sem=send_sem.at[n, s], recv_sem=recv_sem.at[n, u],
            device_id={"uly": s, "blk": b}, device_id_type=MESH,
        )

    def arriving(n, s):
        return pltpu.make_async_remote_copy(
            src_ref=ins[n].at[s], dst_ref=at(bufs[n], s, b),
            send_sem=send_sem.at[n, s], recv_sem=recv_sem.at[n, s],
            device_id={"uly": s, "blk": b}, device_id_type=MESH,
        )

    def across(n, s):
        return pltpu.make_async_remote_copy(
            src_ref=at(bufs[n], s, b), dst_ref=at(bufs[n], s, b),
            send_sem=fsend_sem.at[n, s], recv_sem=frecv_sem.at[n, s],
            device_id={"uly": u, "blk": sib}, device_id_type=MESH,
        )

    def across_in(n, s):
        return pltpu.make_async_remote_copy(
            src_ref=at(bufs[n], s, sib), dst_ref=at(bufs[n], s, sib),
            send_sem=fsend_sem.at[n, s], recv_sem=frecv_sem.at[n, s],
            device_id={"uly": u, "blk": sib}, device_id_type=MESH,
        )

    def own(n):
        return pltpu.make_async_copy(ins[n].at[u], at(bufs[n], u, b), loc_sem.at[n])

    def own_across(n):
        return pltpu.make_async_remote_copy(
            src_ref=ins[n].at[u], dst_ref=at(bufs[n], u, b),
            send_sem=fsend_sem.at[n, u], recv_sem=frecv_sem.at[n, u],
            device_id={"uly": u, "blk": sib}, device_id_type=MESH,
        )

    for n in range(3):
        def push(i, c, n=n):
            away(n, flip(u, U - 1 - i, U)).start()
            return c

        lax.fori_loop(0, U - 1, push, 0)
        own(n).start()
        own_across(n).start()

    def relay(n, s):
        arriving(n, s).wait_recv()
        across(n, s).start()

    for n in range(2):
        def pass_on(i, c, n=n):
            relay(n, flip(u, U - 1 - i, U))
            return c

        lax.fori_loop(0, U - 1, pass_on, 0)
    for n in range(2):
        own(n).wait()

        def take(s, c, n=n):
            across_in(n, s).wait_recv()
            return c

        lax.fori_loop(0, U, take, 0)

    def scores(query, key_rows):
        return lax.dot_general(
            query, key_rows, (((1,), (1,)), ((), ())), preferred_element_type=jnp.float32
        )

    def score_tile(s, i):
        tile = (s * 2 + b) * per + i
        slot = s * per + i
        rows = jnp.concatenate([K[pat[0, tile, j]] for j in range(listed)], axis=0)
        sc = scores(Q[tile], rows)
        top = jnp.max(sc, axis=-1, keepdims=True)
        w = jnp.exp2((sc - top) * c2)
        total[slot] = jnp.broadcast_to(jnp.sum(w, axis=-1, keepdims=True), (TILE, head))
        probs[slot] = w.astype(jnp.bfloat16)

    def score_chunk(c, carry):
        s = flip(u, U - 1 - c, U)
        for i in range(per):
            score_tile(s, i)

        return carry

    def score_and_relay(c, carry):
        score_chunk(c, carry)
        relay(2, flip(u, U - 1 - c, U))
        return carry

    def dense_scores(h):
        query = Q[heavy[0, h]]

        def keys_of(g):
            return K[pl.ds(g * group, group)].reshape(group * TILE, head)

        def top_of(g, top):
            return jnp.maximum(top, jnp.max(scores(query, keys_of(g)), axis=-1, keepdims=True))

        top = lax.fori_loop(
            0, tiles // group, top_of, jnp.full((TILE, 1), -jnp.inf, jnp.float32)
        )

        def weigh(g, acc):
            w = jnp.exp2((scores(query, keys_of(g)) - top) * c2)
            dense_p[h, g] = w.astype(jnp.bfloat16)
            return acc + jnp.sum(w, axis=-1, keepdims=True)

        acc = lax.fori_loop(0, tiles // group, weigh, jnp.zeros((TILE, 1), jnp.float32))
        dense_o[h] = jnp.broadcast_to(acc, (TILE, head))

    for h in range(heavies):
        dense_scores(h)
    lax.fori_loop(0, U - 1, score_and_relay, 0)
    score_chunk(U - 1, 0)

    own(2).wait()

    def take_v(s, c):
        across_in(2, s).wait_recv()
        return c

    lax.fori_loop(0, U, take_v, 0)

    for h in range(heavies):
        def blend(g, acc, h=h):
            rows = V[pl.ds(g * group, group)].reshape(group * TILE, head)
            return acc + jnp.dot(dense_p[h, g], rows, preferred_element_type=jnp.float32)

        acc = lax.fori_loop(0, tiles // group, blend, jnp.zeros((TILE, head), jnp.float32))
        dense_o[h] = acc / dense_o[h]

    def back(s):
        return pltpu.make_async_remote_copy(
            src_ref=o_send.at[s], dst_ref=out.at[u],
            send_sem=osend_sem.at[s], recv_sem=orecv_sem.at[u],
            device_id={"uly": s, "blk": b}, device_id_type=MESH,
        )

    def back_in(s):
        return pltpu.make_async_remote_copy(
            src_ref=o_send.at[s], dst_ref=out.at[s],
            send_sem=osend_sem.at[s], recv_sem=orecv_sem.at[s],
            device_id={"uly": s, "blk": b}, device_id_type=MESH,
        )

    def finish(s):
        for i in range(per):
            tile = (s * 2 + b) * per + i
            slot = s * per + i
            rows = jnp.concatenate([V[pat[0, tile, j]] for j in range(listed)], axis=0)
            res = jnp.dot(probs[slot], rows, preferred_element_type=jnp.float32) / total[slot]
            for h in range(heavies):
                res = jnp.where(heavy[0, h] == tile, dense_o[h], res)
            o_send[s, i] = res.astype(jnp.bfloat16)

    def finish_chunk(c, carry):
        s = flip(u, U - 1 - c, U)
        finish(s)
        back(s).start()
        return carry

    lax.fori_loop(0, U - 1, finish_chunk, 0)
    finish(u)
    mine = pltpu.make_async_copy(o_send.at[u], out.at[u], loc_sem.at[3])
    mine.start()
    mine.wait()

    def close(i, c):
        s = flip(u, i + 1, U)
        for n in range(3):
            away(n, s).wait_send()
            across(n, s).wait_send()
        back(s).wait_send()
        back_in(s).wait_recv()
        return c

    lax.fori_loop(0, U - 1, close, 0)
    for n in range(3):
        own_across(n).wait_send()


def per_device(queries, keys, values, pattern, heavy):
    tokens, heads, head = queries.shape
    U = lax.axis_size("uly")
    per = tokens // TILE
    tiles = U * 2 * per
    group = math.gcd(tiles, 8)
    listed, heavies = pattern.shape[2], heavy.shape[1]

    def by_head(x):
        return x.transpose(1, 0, 2).reshape(heads, per, TILE, head)

    bf = jnp.bfloat16
    any_ = pl.BlockSpec(memory_space=pl.ANY)
    smem = pl.BlockSpec(memory_space=pltpu.SMEM)
    dma = pltpu.SemaphoreType.DMA
    done = pl.pallas_call(
        functools.partial(kernel, U, per),
        out_shape=jax.ShapeDtypeStruct((heads, per, TILE, head), bf),
        in_specs=[smem, smem, any_, any_, any_],
        out_specs=any_,
        scratch_shapes=[
            pltpu.VMEM((tiles, TILE, head), bf),
            pltpu.VMEM((tiles, TILE, head), bf),
            pltpu.VMEM((tiles, TILE, head), bf),
            pltpu.VMEM((tiles // 2, TILE, listed * TILE), bf),
            pltpu.VMEM((tiles // 2, TILE, head), jnp.float32),
            pltpu.VMEM((heavies, tiles // group, TILE, group * TILE), bf),
            pltpu.VMEM((heavies, TILE, head), jnp.float32),
            pltpu.VMEM((U, per, TILE, head), bf),
            dma((3, U)), dma((3, U)), dma((3, U)), dma((3, U)), dma((4,)), dma((U,)), dma((U,)),
        ],
        compiler_params=pltpu.CompilerParams(
            collective_id=0, has_side_effects=True, vmem_limit_bytes=56 * 2 ** 20
        ),
    )(pattern, heavy, by_head(queries), by_head(keys), by_head(values))
    return done.reshape(heads, tokens, head).transpose(1, 0, 2)


def solution(mesh):
    rows = P(("grp", "uly", "blk"), None, None)
    placed = (rows, rows, rows, P(("grp", "uly"), None, None), P(("grp", "uly"), None))
    return jax.shard_map(
        per_device, mesh=mesh, in_specs=placed, out_specs=rows, check_vma=False,
    )
```

```python
import functools
import math

import jax
import jax.numpy as jnp
from jax import lax
from jax.experimental import pallas as pl
from jax.experimental.pallas import tpu as pltpu
from jax.sharding import PartitionSpec as P

TILE = 128
MESH = pl.DeviceIdType.MESH


def flip(u, d, count):
    if count & (count - 1):
        return (d + count - u) % count
    out, k = 0, 1
    while k < count:
        out = out + ((u // k + d // k) % 2) * k
        k *= 2
    return out


def kernel(
    U, per, pat_in, heavy_in, q_in, k_in, v_in, out,
    Q, K, V, probs, total, dense_p, dense_o, o_send, pat, heavy, staged, wide, k_s, q_s, v_s,
    send_sem, recv_sem, fsend_sem, frecv_sem, loc_sem, osend_sem, orecv_sem, in_sem,
):
    u, b = lax.axis_index("uly"), lax.axis_index("blk")
    sib = 1 - b
    tiles, head = K.shape[0], K.shape[2]
    listed, heavies = pat.shape[2], heavy.shape[1]
    c2 = head ** (-0.5) * math.log2(math.e)
    group = 2 * per
    bufs, ins = (K, Q, V), (k_s, q_s, v_s)
    heads = staged.shape[2]

    barrier = pltpu.get_barrier_semaphore()

    def greet(d, c):
        pl.semaphore_signal(
            barrier, inc=1, device_id={"uly": flip(u, d, U), "blk": b}, device_id_type=MESH
        )
        return c

    lax.fori_loop(1, U, greet, 0)
    pl.semaphore_signal(barrier, inc=1, device_id={"uly": u, "blk": sib}, device_id_type=MESH)

    def fetch(n):
        return pltpu.make_async_copy((k_in, q_in, v_in)[n], staged.at[n], in_sem.at[n])

    tables = (
        pltpu.make_async_copy(pat_in, pat, in_sem.at[3]),
        pltpu.make_async_copy(heavy_in, heavy, in_sem.at[4]),
    )
    for n in range(3):
        fetch(n).start()
    for copy in tables:
        copy.start()

    def widen(n):
        fetch(n).wait()
        for r in range(per):
            rows = staged[n, r * TILE:(r + 1) * TILE].astype(jnp.float32)
            wide[r] = rows.reshape(TILE * heads, head)

    def split(n, s):
        for r in range(per):
            ins[n][s, r] = wide[r, pl.ds(s, TILE, stride=heads), :].astype(jnp.bfloat16)

    def split_all(s, c):
        split(0, s)
        return c

    widen(0)
    lax.fori_loop(0, U, split_all, 0)
    pl.semaphore_wait(barrier, U)

    def at(buf, s, half):
        return buf.at[pl.ds((s * 2 + half) * per, per)]

    def away(n, s):
        return pltpu.make_async_remote_copy(
            src_ref=ins[n].at[s], dst_ref=at(bufs[n], u, b),
            send_sem=send_sem.at[n, s], recv_sem=recv_sem.at[n, u],
            device_id={"uly": s, "blk": b}, device_id_type=MESH,
        )

    def arriving(n, s):
        return pltpu.make_async_remote_copy(
            src_ref=ins[n].at[s], dst_ref=at(bufs[n], s, b),
            send_sem=send_sem.at[n, s], recv_sem=recv_sem.at[n, s],
            device_id={"uly": s, "blk": b}, device_id_type=MESH,
        )

    def across(n, s):
        return pltpu.make_async_remote_copy(
            src_ref=at(bufs[n], s, b), dst_ref=at(bufs[n], s, b),
            send_sem=fsend_sem.at[n, s], recv_sem=frecv_sem.at[n, s],
            device_id={"uly": u, "blk": sib}, device_id_type=MESH,
        )

    def across_in(n, s):
        return pltpu.make_async_remote_copy(
            src_ref=at(bufs[n], s, sib), dst_ref=at(bufs[n], s, sib),
            send_sem=fsend_sem.at[n, s], recv_sem=frecv_sem.at[n, s],
            device_id={"uly": u, "blk": sib}, device_id_type=MESH,
        )

    def own(n):
        return pltpu.make_async_copy(ins[n].at[u], at(bufs[n], u, b), loc_sem.at[n])

    def own_across(n):
        return pltpu.make_async_remote_copy(
            src_ref=ins[n].at[u], dst_ref=at(bufs[n], u, b),
            send_sem=fsend_sem.at[n, u], recv_sem=frecv_sem.at[n, u],
            device_id={"uly": u, "blk": sib}, device_id_type=MESH,
        )

    for n in range(3):
        def push(i, c, n=n):
            s = flip(u, U - 1 - i, U)
            if n:
                split(n, s)
            away(n, s).start()
            return c

        if n:
            widen(n)
        lax.fori_loop(0, U - 1, push, 0)
        if n:
            split(n, u)
        own(n).start()
        own_across(n).start()

    def relay(n, s):
        arriving(n, s).wait_recv()
        across(n, s).start()

    def pass_on(i, c):
        relay(0, flip(u, U - 1 - i, U))
        return c

    lax.fori_loop(0, U - 1, pass_on, 0)
    own(0).wait()
    own(1).wait()
    for copy in tables:
        copy.wait()

    def take(s, c, n=0):
        across_in(n, s).wait_recv()
        return c

    lax.fori_loop(0, U, take, 0)

    def scores(query, key_rows):
        return lax.dot_general(
            query, key_rows, (((1,), (1,)), ((), ())), preferred_element_type=jnp.float32
        )

    def score_tile(s, i):
        tile = (s * 2 + b) * per + i
        slot = s * per + i
        rows = jnp.concatenate([K[pat[0, tile, j]] for j in range(listed)], axis=0)
        sc = scores(Q[tile], rows)
        top = jnp.max(sc, axis=-1, keepdims=True)
        w = jnp.exp2((sc - top) * c2)
        total[slot] = jnp.broadcast_to(jnp.sum(w, axis=-1, keepdims=True), (TILE, head))
        probs[slot] = w.astype(jnp.bfloat16)

    def score_chunk(c, carry):
        s = flip(u, U - 1 - c, U)
        for i in range(per):
            score_tile(s, i)

        return carry

    def relay_and_score(c, carry):
        relay(1, flip(u, U - 1 - c, U))
        return score_chunk(c, carry)

    def dense_scores(h):
        query = Q[heavy[0, h]]

        def keys_of(g):
            return K[pl.ds(g * group, group)].reshape(group * TILE, head)

        def top_of(g, top):
            return jnp.maximum(top, jnp.max(scores(query, keys_of(g)), axis=-1, keepdims=True))

        top = lax.fori_loop(
            0, tiles // group, top_of, jnp.full((TILE, 1), -jnp.inf, jnp.float32)
        )

        def weigh(g, acc):
            w = jnp.exp2((scores(query, keys_of(g)) - top) * c2)
            dense_p[h, g] = w.astype(jnp.bfloat16)
            return acc + jnp.sum(w, axis=-1, keepdims=True)

        acc = lax.fori_loop(0, tiles // group, weigh, jnp.zeros((TILE, 1), jnp.float32))
        dense_o[h] = jnp.broadcast_to(acc, (TILE, head))

    score_chunk(U - 1, 0)
    lax.fori_loop(0, U - 1, relay_and_score, 0)
    lax.fori_loop(0, U, functools.partial(take, n=1), 0)
    for h in range(heavies):
        dense_scores(h)
    own(2).wait()

    def blend(s, accs):
        rows = V[pl.ds(s * 2 * per, 2 * per)].reshape(2 * per * TILE, head)
        return tuple(
            acc + jnp.dot(dense_p[h, s], rows, preferred_element_type=jnp.float32)
            for h, acc in enumerate(accs)
        )

    def relay_and_blend(c, accs):
        s = flip(u, U - 1 - c, U)
        relay(2, s)
        before = jnp.where(c == 0, u, flip(u, U - c, U))
        across_in(2, before).wait_recv()
        return blend(before, accs)

    accs = tuple(jnp.zeros((TILE, head), jnp.float32) for _ in range(heavies))
    accs = lax.fori_loop(0, U - 1, relay_and_blend, accs)
    last = flip(u, 1, U)
    across_in(2, last).wait_recv()
    for h, acc in enumerate(blend(last, accs)):
        dense_o[h] = acc / dense_o[h]

    def back(s):
        return pltpu.make_async_remote_copy(
            src_ref=o_send.at[s], dst_ref=out.at[u],
            send_sem=osend_sem.at[s], recv_sem=orecv_sem.at[u],
            device_id={"uly": s, "blk": b}, device_id_type=MESH,
        )

    def back_in(s):
        return pltpu.make_async_remote_copy(
            src_ref=o_send.at[s], dst_ref=out.at[s],
            send_sem=osend_sem.at[s], recv_sem=orecv_sem.at[s],
            device_id={"uly": s, "blk": b}, device_id_type=MESH,
        )

    def finish(s):
        for i in range(per):
            tile = (s * 2 + b) * per + i
            slot = s * per + i
            rows = jnp.concatenate([V[pat[0, tile, j]] for j in range(listed)], axis=0)
            res = jnp.dot(probs[slot], rows, preferred_element_type=jnp.float32) / total[slot]
            for h in range(heavies):
                res = jnp.where(heavy[0, h] == tile, dense_o[h], res)
            o_send[s, i] = res.astype(jnp.bfloat16)

    def finish_chunk(c, carry):
        s = flip(u, U - 1 - c, U)
        finish(s)
        back(s).start()
        return carry

    lax.fori_loop(0, U - 1, finish_chunk, 0)
    finish(u)
    mine = pltpu.make_async_copy(o_send.at[u], out.at[u], loc_sem.at[3])
    mine.start()
    mine.wait()

    def close(i, c):
        s = flip(u, i + 1, U)
        for n in range(3):
            away(n, s).wait_send()
            across(n, s).wait_send()
        back(s).wait_send()
        back_in(s).wait_recv()
        return c

    lax.fori_loop(0, U - 1, close, 0)
    for n in range(3):
        own_across(n).wait_send()


def per_device(queries, keys, values, pattern, heavy):
    tokens, heads, head = queries.shape
    U = lax.axis_size("uly")
    per = tokens // TILE
    tiles = U * 2 * per
    group = 2 * per
    listed, heavies = pattern.shape[2], heavy.shape[1]


    bf = jnp.bfloat16
    any_ = pl.BlockSpec(memory_space=pl.ANY)
    dma = pltpu.SemaphoreType.DMA
    done = pl.pallas_call(
        functools.partial(kernel, U, per),
        out_shape=jax.ShapeDtypeStruct((heads, per, TILE, head), bf),
        in_specs=[any_] * 5,
        out_specs=any_,
        scratch_shapes=[
            pltpu.VMEM((tiles, TILE, head), bf),
            pltpu.VMEM((tiles, TILE, head), bf),
            pltpu.VMEM((tiles, TILE, head), bf),
            pltpu.VMEM((tiles // 2, TILE, listed * TILE), bf),
            pltpu.VMEM((tiles // 2, TILE, head), jnp.float32),
            pltpu.VMEM((heavies, tiles // group, TILE, group * TILE), bf),
            pltpu.VMEM((heavies, TILE, head), jnp.float32),
            pltpu.VMEM((U, per, TILE, head), bf),
            pltpu.SMEM(pattern.shape, jnp.int32),
            pltpu.SMEM(heavy.shape, jnp.int32),
            pltpu.VMEM((3, tokens, heads, head), bf),
            pltpu.VMEM((per, TILE * heads, head), jnp.float32),
            *[pltpu.VMEM((U, per, TILE, head), bf)] * 3,
            dma((3, U)), dma((3, U)), dma((3, U)), dma((3, U)), dma((4,)), dma((U,)), dma((U,)), dma((5,)),
        ],
        compiler_params=pltpu.CompilerParams(
            collective_id=0, has_side_effects=True, vmem_limit_bytes=60 * 2 ** 20
        ),
    )(pattern, heavy, queries, keys, values)
    return done.reshape(heads, tokens, head).transpose(1, 0, 2)


def solution(mesh):
    rows = P(("grp", "uly", "blk"), None, None)
    placed = (rows, rows, rows, P(("grp", "uly"), None, None), P(("grp", "uly"), None))
    return jax.shard_map(
        per_device, mesh=mesh, in_specs=placed, out_specs=rows, check_vma=False,
    )
```

```python
import functools
import math

import jax
import jax.numpy as jnp
from jax import lax
from jax.experimental import pallas as pl
from jax.experimental.pallas import tpu as pltpu
from jax.sharding import PartitionSpec as P

TILE = 128
MESH = pl.DeviceIdType.MESH


def flip(u, d, count):
    if count & (count - 1):
        return (d + count - u) % count
    out, k = 0, 1
    while k < count:
        out = out + ((u // k + d // k) % 2) * k
        k *= 2
    return out


def kernel(
    U, per, pat_in, heavy_in, q_in, k_in, v_in, out,
    Q, K, V, probs, total, dense_p, dense_o, o_send, pat, heavy, staged, wide, k_s, q_s, v_s,
    send_sem, recv_sem, fsend_sem, frecv_sem, loc_sem, osend_sem, orecv_sem, in_sem,
):
    u, b = lax.axis_index("uly"), lax.axis_index("blk")
    sib = 1 - b
    tiles, head = K.shape[0], K.shape[2]
    listed, heavies = pat.shape[2], heavy.shape[1]
    c2 = head ** (-0.5) * math.log2(math.e)
    group = 2 * per
    bufs, ins = (K, Q, V), (k_s, q_s, v_s)
    heads = staged.shape[2]

    barrier = pltpu.get_barrier_semaphore()

    def greet(d, c):
        pl.semaphore_signal(
            barrier, inc=1, device_id={"uly": flip(u, d, U), "blk": b}, device_id_type=MESH
        )
        return c

    lax.fori_loop(1, U, greet, 0)
    pl.semaphore_signal(barrier, inc=1, device_id={"uly": u, "blk": sib}, device_id_type=MESH)

    def fetch(n):
        return pltpu.make_async_copy((k_in, q_in, v_in)[n], staged.at[n], in_sem.at[n])

    tables = (
        pltpu.make_async_copy(pat_in, pat, in_sem.at[3]),
        pltpu.make_async_copy(heavy_in, heavy, in_sem.at[4]),
    )
    for n in range(3):
        fetch(n).start()
    for copy in tables:
        copy.start()

    def widen(n):
        fetch(n).wait()
        for r in range(per):
            rows = staged[n, r * TILE:(r + 1) * TILE].astype(jnp.float32)
            wide[r] = rows.reshape(TILE * heads, head)

    def split(n, s):
        for r in range(per):
            ins[n][s, r] = wide[r, pl.ds(s, TILE, stride=heads), :].astype(jnp.bfloat16)

    def split_all(s, c):
        split(0, s)
        return c

    widen(0)
    lax.fori_loop(0, U, split_all, 0)
    pl.semaphore_wait(barrier, U)

    def at(buf, s, half):
        return buf.at[pl.ds((s * 2 + half) * per, per)]

    def away(n, s):
        return pltpu.make_async_remote_copy(
            src_ref=ins[n].at[s], dst_ref=at(bufs[n], u, b),
            send_sem=send_sem.at[n, s], recv_sem=recv_sem.at[n, u],
            device_id={"uly": s, "blk": b}, device_id_type=MESH,
        )

    def arriving(n, s):
        return pltpu.make_async_remote_copy(
            src_ref=ins[n].at[s], dst_ref=at(bufs[n], s, b),
            send_sem=send_sem.at[n, s], recv_sem=recv_sem.at[n, s],
            device_id={"uly": s, "blk": b}, device_id_type=MESH,
        )

    def across(n, s):
        return pltpu.make_async_remote_copy(
            src_ref=at(bufs[n], s, b), dst_ref=at(bufs[n], s, b),
            send_sem=fsend_sem.at[n, s], recv_sem=frecv_sem.at[n, s],
            device_id={"uly": u, "blk": sib}, device_id_type=MESH,
        )

    def across_in(n, s):
        return pltpu.make_async_remote_copy(
            src_ref=at(bufs[n], s, sib), dst_ref=at(bufs[n], s, sib),
            send_sem=fsend_sem.at[n, s], recv_sem=frecv_sem.at[n, s],
            device_id={"uly": u, "blk": sib}, device_id_type=MESH,
        )

    def own(n):
        return pltpu.make_async_copy(ins[n].at[u], at(bufs[n], u, b), loc_sem.at[n])

    def own_across(n):
        return pltpu.make_async_remote_copy(
            src_ref=ins[n].at[u], dst_ref=at(bufs[n], u, b),
            send_sem=fsend_sem.at[n, u], recv_sem=frecv_sem.at[n, u],
            device_id={"uly": u, "blk": sib}, device_id_type=MESH,
        )

    for n in range(3):
        def push(i, c, n=n):
            s = flip(u, U - 1 - i, U)
            if n:
                split(n, s)
            away(n, s).start()
            return c

        if n:
            widen(n)
        lax.fori_loop(0, U - 1, push, 0)
        if n:
            split(n, u)
        own(n).start()
        own_across(n).start()

    def relay(n, s):
        arriving(n, s).wait_recv()
        across(n, s).start()

    def pass_on(i, c):
        relay(0, flip(u, U - 1 - i, U))
        return c

    lax.fori_loop(0, U - 1, pass_on, 0)
    own(0).wait()
    own(1).wait()
    for copy in tables:
        copy.wait()

    def take(s, c, n=0):
        across_in(n, s).wait_recv()
        return c

    lax.fori_loop(0, U, take, 0)

    def scores(query, key_rows):
        return lax.dot_general(
            query, key_rows, (((1,), (1,)), ((), ())), preferred_element_type=jnp.float32
        )

    def score_tile(s, i):
        tile = (s * 2 + b) * per + i
        slot = s * per + i
        rows = jnp.concatenate([K[pat[0, tile, j]] for j in range(listed)], axis=0)
        sc = scores(Q[tile], rows)
        top = jnp.max(fold(jnp.maximum, sc), axis=-1, keepdims=True)
        w = jnp.exp2((sc - top) * c2)
        total[slot] = jnp.broadcast_to(jnp.sum(fold(jnp.add, w), axis=-1, keepdims=True), (TILE, head))
        probs[slot] = w.astype(jnp.bfloat16)

    def score_chunk(c, carry):
        s = flip(u, U - 1 - c, U)
        for i in range(per):
            score_tile(s, i)

        return carry

    def relay_and_score(c, carry):
        relay(1, flip(u, U - 1 - c, U))
        return score_chunk(c, carry)

    def fold(op, x):
        parts = [x[:, k * head:(k + 1) * head] for k in range(x.shape[1] // head)]
        while len(parts) > 1:
            parts = [op(*parts[k:k + 2]) if k + 1 < len(parts) else parts[k]
                     for k in range(0, len(parts), 2)]
        return parts[0]

    def dense_scores():
        steps = tiles // group
        asked = [Q[heavy[0, h]] for h in range(heavies)]

        def keys_of(g):
            return K[pl.ds(g * group, group)].reshape(group * TILE, head)

        def top_of(g, tops):
            rows = keys_of(g)
            return tuple(
                jnp.maximum(top, fold(jnp.maximum, scores(query, rows)))
                for query, top in zip(asked, tops)
            )

        tops = lax.fori_loop(
            0, steps, top_of, (jnp.full((TILE, head), -jnp.inf, jnp.float32),) * heavies,
            unroll=math.gcd(steps, 4),
        )
        tops = [jnp.max(top, axis=-1, keepdims=True) for top in tops]

        def weigh(g, accs):
            rows, new = keys_of(g), []
            for h in range(heavies):
                w = jnp.exp2((scores(asked[h], rows) - tops[h]) * c2)
                dense_p[h, g] = w.astype(jnp.bfloat16)
                new.append(accs[h] + fold(jnp.add, w))
            return tuple(new)

        accs = lax.fori_loop(
            0, steps, weigh, (jnp.zeros((TILE, head), jnp.float32),) * heavies,
            unroll=math.gcd(steps, 4),
        )
        for h in range(heavies):
            dense_o[h] = jnp.broadcast_to(
                jnp.sum(accs[h], axis=-1, keepdims=True), (TILE, head)
            )

    score_chunk(U - 1, 0)
    lax.fori_loop(0, U - 1, relay_and_score, 0)
    lax.fori_loop(0, U, functools.partial(take, n=1), 0)
    dense_scores()
    own(2).wait()

    def blend(s, accs):
        rows = V[pl.ds(s * 2 * per, 2 * per)].reshape(2 * per * TILE, head)
        return tuple(
            acc + jnp.dot(dense_p[h, s], rows, preferred_element_type=jnp.float32)
            for h, acc in enumerate(accs)
        )

    def relay_and_blend(c, accs):
        s = flip(u, U - 1 - c, U)
        relay(2, s)
        before = jnp.where(c == 0, u, flip(u, U - c, U))
        across_in(2, before).wait_recv()
        return blend(before, accs)

    accs = tuple(jnp.zeros((TILE, head), jnp.float32) for _ in range(heavies))
    accs = lax.fori_loop(0, U - 1, relay_and_blend, accs)
    last = flip(u, 1, U)
    across_in(2, last).wait_recv()
    for h, acc in enumerate(blend(last, accs)):
        dense_o[h] = acc / dense_o[h]

    def back(s):
        return pltpu.make_async_remote_copy(
            src_ref=o_send.at[s], dst_ref=out.at[u],
            send_sem=osend_sem.at[s], recv_sem=orecv_sem.at[u],
            device_id={"uly": s, "blk": b}, device_id_type=MESH,
        )

    def back_in(s):
        return pltpu.make_async_remote_copy(
            src_ref=o_send.at[s], dst_ref=out.at[s],
            send_sem=osend_sem.at[s], recv_sem=orecv_sem.at[s],
            device_id={"uly": s, "blk": b}, device_id_type=MESH,
        )

    def finish(s):
        for i in range(per):
            tile = (s * 2 + b) * per + i
            slot = s * per + i
            rows = jnp.concatenate([V[pat[0, tile, j]] for j in range(listed)], axis=0)
            res = jnp.dot(probs[slot], rows, preferred_element_type=jnp.float32) / total[slot]
            for h in range(heavies):
                res = jnp.where(heavy[0, h] == tile, dense_o[h], res)
            o_send[s, i] = res.astype(jnp.bfloat16)

    def finish_chunk(c, carry):
        s = flip(u, U - 1 - c, U)
        finish(s)
        back(s).start()
        return carry

    lax.fori_loop(0, U - 1, finish_chunk, 0)
    finish(u)
    mine = pltpu.make_async_copy(o_send.at[u], out.at[u], loc_sem.at[3])
    mine.start()
    mine.wait()

    def close(i, c):
        s = flip(u, i + 1, U)
        for n in range(3):
            away(n, s).wait_send()
            across(n, s).wait_send()
        back(s).wait_send()
        back_in(s).wait_recv()
        return c

    lax.fori_loop(0, U - 1, close, 0)
    for n in range(3):
        own_across(n).wait_send()


def per_device(queries, keys, values, pattern, heavy):
    tokens, heads, head = queries.shape
    U = lax.axis_size("uly")
    per = tokens // TILE
    tiles = U * 2 * per
    group = 2 * per
    listed, heavies = pattern.shape[2], heavy.shape[1]


    bf = jnp.bfloat16
    any_ = pl.BlockSpec(memory_space=pl.ANY)
    dma = pltpu.SemaphoreType.DMA
    done = pl.pallas_call(
        functools.partial(kernel, U, per),
        out_shape=jax.ShapeDtypeStruct((heads, per, TILE, head), bf),
        in_specs=[any_] * 5,
        out_specs=any_,
        scratch_shapes=[
            pltpu.VMEM((tiles, TILE, head), bf),
            pltpu.VMEM((tiles, TILE, head), bf),
            pltpu.VMEM((tiles, TILE, head), bf),
            pltpu.VMEM((tiles // 2, TILE, listed * TILE), bf),
            pltpu.VMEM((tiles // 2, TILE, head), jnp.float32),
            pltpu.VMEM((heavies, tiles // group, TILE, group * TILE), bf),
            pltpu.VMEM((heavies, TILE, head), jnp.float32),
            pltpu.VMEM((U, per, TILE, head), bf),
            pltpu.SMEM(pattern.shape, jnp.int32),
            pltpu.SMEM(heavy.shape, jnp.int32),
            pltpu.VMEM((3, tokens, heads, head), bf),
            pltpu.VMEM((per, TILE * heads, head), jnp.float32),
            *[pltpu.VMEM((U, per, TILE, head), bf)] * 3,
            dma((3, U)), dma((3, U)), dma((3, U)), dma((3, U)), dma((4,)), dma((U,)), dma((U,)), dma((5,)),
        ],
        compiler_params=pltpu.CompilerParams(
            collective_id=0, has_side_effects=True, vmem_limit_bytes=60 * 2 ** 20
        ),
    )(pattern, heavy, queries, keys, values)
    return done.reshape(heads, tokens, head).transpose(1, 0, 2)


def solution(mesh):
    rows = P(("grp", "uly", "blk"), None, None)
    placed = (rows, rows, rows, P(("grp", "uly"), None, None), P(("grp", "uly"), None))
    return jax.shard_map(
        per_device, mesh=mesh, in_specs=placed, out_specs=rows, check_vma=False,
    )
```

```python
import functools
import math

import jax
import jax.numpy as jnp
from jax import lax
from jax.experimental import pallas as pl
from jax.experimental.pallas import tpu as pltpu
from jax.sharding import PartitionSpec as P

TILE = 128
MESH = pl.DeviceIdType.MESH


def flip(u, d, count):
    if count & (count - 1):
        return (d + count - u) % count
    out, k = 0, 1
    while k < count:
        out = out + ((u // k + d // k) % 2) * k
        k *= 2
    return out


def kernel(
    U, per, pat_in, heavy_in, q_in, k_in, v_in, out,
    Q, K, V, probs, total, dense_p, dense_o, pat, heavy, staged, wide, k_s, q_s, v_s, o_got,
    send_sem, recv_sem, fsend_sem, frecv_sem, loc_sem, osend_sem, orecv_sem, in_sem,
):
    u, b = lax.axis_index("uly"), lax.axis_index("blk")
    sib = 1 - b
    tiles, head = K.shape[0], K.shape[2]
    listed, heavies = pat.shape[1], heavy.shape[1]
    c2 = head ** (-0.5) * math.log2(math.e)
    group = 2 * per
    bufs, ins = (K, Q, V), (k_s, q_s, v_s)
    heads = staged.shape[2]
    o_send = k_s

    barrier = pltpu.get_barrier_semaphore()

    def greet(d, c):
        pl.semaphore_signal(
            barrier, inc=1, device_id={"uly": flip(u, d, U), "blk": b}, device_id_type=MESH
        )
        return c

    lax.fori_loop(1, U, greet, 0)
    pl.semaphore_signal(barrier, inc=1, device_id={"uly": u, "blk": sib}, device_id_type=MESH)

    def fetch(n):
        return pltpu.make_async_copy((k_in, q_in, v_in)[n], staged.at[n], in_sem.at[n])

    tables = (
        pltpu.make_async_copy(pat_in, pat, in_sem.at[3]),
        pltpu.make_async_copy(heavy_in, heavy, in_sem.at[4]),
    )
    for n in range(3):
        fetch(n).start()
    for copy in tables:
        copy.start()

    def widen(n):
        fetch(n).wait()
        for r in range(per):
            rows = staged[n, r * TILE:(r + 1) * TILE].astype(jnp.float32)
            wide[r] = rows.reshape(TILE * heads, head)

    def split(n, s):
        for r in range(per):
            ins[n][s, r] = wide[r, pl.ds(s, TILE, stride=heads), :].astype(jnp.bfloat16)

    def split_all(s, c):
        split(0, s)
        return c

    widen(0)
    lax.fori_loop(0, U, split_all, 0)
    pl.semaphore_wait(barrier, U)

    def at(buf, s, half):
        return buf.at[pl.ds((s * 2 + half) * per, per)]

    def away(n, s):
        return pltpu.make_async_remote_copy(
            src_ref=ins[n].at[s], dst_ref=at(bufs[n], u, b),
            send_sem=send_sem.at[n, s], recv_sem=recv_sem.at[n, u],
            device_id={"uly": s, "blk": b}, device_id_type=MESH,
        )

    def arriving(n, s):
        return pltpu.make_async_remote_copy(
            src_ref=ins[n].at[s], dst_ref=at(bufs[n], s, b),
            send_sem=send_sem.at[n, s], recv_sem=recv_sem.at[n, s],
            device_id={"uly": s, "blk": b}, device_id_type=MESH,
        )

    def across(n, s):
        return pltpu.make_async_remote_copy(
            src_ref=at(bufs[n], s, b), dst_ref=at(bufs[n], s, b),
            send_sem=fsend_sem.at[n, s], recv_sem=frecv_sem.at[n, s],
            device_id={"uly": u, "blk": sib}, device_id_type=MESH,
        )

    def across_in(n, s):
        return pltpu.make_async_remote_copy(
            src_ref=at(bufs[n], s, sib), dst_ref=at(bufs[n], s, sib),
            send_sem=fsend_sem.at[n, s], recv_sem=frecv_sem.at[n, s],
            device_id={"uly": u, "blk": sib}, device_id_type=MESH,
        )

    def own(n):
        return pltpu.make_async_copy(ins[n].at[u], at(bufs[n], u, b), loc_sem.at[n])

    def own_across(n):
        return pltpu.make_async_remote_copy(
            src_ref=ins[n].at[u], dst_ref=at(bufs[n], u, b),
            send_sem=fsend_sem.at[n, u], recv_sem=frecv_sem.at[n, u],
            device_id={"uly": u, "blk": sib}, device_id_type=MESH,
        )

    for n in range(3):
        def push(i, c, n=n):
            s = flip(u, U - 1 - i, U)
            if n:
                split(n, s)
            away(n, s).start()
            return c

        if n:
            widen(n)
        lax.fori_loop(0, U - 1, push, 0)
        if n:
            split(n, u)
        own(n).start()
        own_across(n).start()

    def relay(n, s):
        arriving(n, s).wait_recv()
        across(n, s).start()

    def pass_on(i, c):
        relay(0, flip(u, U - 1 - i, U))
        return c

    lax.fori_loop(0, U - 1, pass_on, 0)
    own(0).wait()
    own(1).wait()
    for copy in tables:
        copy.wait()

    def take(s, c, n=0):
        across_in(n, s).wait_recv()
        return c

    lax.fori_loop(0, U, take, 0)

    def scores(query, key_rows):
        return lax.dot_general(
            query, key_rows, (((1,), (1,)), ((), ())), preferred_element_type=jnp.float32
        )

    def score_tile(s, i):
        tile = (s * 2 + b) * per + i
        slot = s * per + i
        rows = jnp.concatenate([K[pat[0, j, tile]] for j in range(listed)], axis=0)
        sc = scores(Q[tile], rows)
        top = jnp.max(fold(jnp.maximum, sc), axis=-1, keepdims=True)
        w = jnp.exp2((sc - top) * c2)
        total[slot] = jnp.broadcast_to(jnp.sum(fold(jnp.add, w), axis=-1, keepdims=True), (TILE, head))
        probs[slot] = w.astype(jnp.bfloat16)

    def score_chunk(c, carry):
        s = flip(u, U - 1 - c, U)
        for i in range(per):
            score_tile(s, i)

        return carry

    def relay_and_score(c, carry):
        relay(1, flip(u, U - 1 - c, U))
        return score_chunk(c, carry)

    def fold(op, x):
        parts = [x[:, k * head:(k + 1) * head] for k in range(x.shape[1] // head)]
        while len(parts) > 1:
            parts = [op(*parts[k:k + 2]) if k + 1 < len(parts) else parts[k]
                     for k in range(0, len(parts), 2)]
        return parts[0]

    def dense_scores():
        steps = tiles // group
        asked = [Q[heavy[0, h]] for h in range(heavies)]

        def keys_of(g):
            return K[pl.ds(g * group, group)].reshape(group * TILE, head)

        def top_of(g, tops):
            rows = keys_of(g)
            return tuple(
                jnp.maximum(top, fold(jnp.maximum, scores(query, rows)))
                for query, top in zip(asked, tops)
            )

        tops = lax.fori_loop(
            0, steps, top_of, (jnp.full((TILE, head), -jnp.inf, jnp.float32),) * heavies,
            unroll=math.gcd(steps, 4),
        )
        tops = [jnp.max(top, axis=-1, keepdims=True) for top in tops]

        def weigh(g, accs):
            rows, new = keys_of(g), []
            for h in range(heavies):
                w = jnp.exp2((scores(asked[h], rows) - tops[h]) * c2)
                dense_p[h, g] = w.astype(jnp.bfloat16)
                new.append(accs[h] + fold(jnp.add, w))
            return tuple(new)

        accs = lax.fori_loop(
            0, steps, weigh, (jnp.zeros((TILE, head), jnp.float32),) * heavies,
            unroll=math.gcd(steps, 4),
        )
        for h in range(heavies):
            dense_o[h] = jnp.broadcast_to(
                jnp.sum(accs[h], axis=-1, keepdims=True), (TILE, head)
            )

    def sent_keys(i, c):
        s = flip(u, i + 1, U)
        away(0, s).wait_send()
        return c

    lax.fori_loop(0, U - 1, sent_keys, 0)
    own_across(0).wait_send()
    score_chunk(U - 1, 0)
    lax.fori_loop(0, U - 1, relay_and_score, 0)
    lax.fori_loop(0, U, functools.partial(take, n=1), 0)
    dense_scores()
    own(2).wait()

    def blend(s, accs):
        rows = V[pl.ds(s * 2 * per, 2 * per)].reshape(2 * per * TILE, head)
        return tuple(
            acc + jnp.dot(dense_p[h, s], rows, preferred_element_type=jnp.float32)
            for h, acc in enumerate(accs)
        )

    def relay_and_blend(c, accs):
        s = flip(u, U - 1 - c, U)
        relay(2, s)
        before = jnp.where(c == 0, u, flip(u, U - c, U))
        across_in(2, before).wait_recv()
        return blend(before, accs)

    accs = tuple(jnp.zeros((TILE, head), jnp.float32) for _ in range(heavies))
    accs = lax.fori_loop(0, U - 1, relay_and_blend, accs)
    last = flip(u, 1, U)
    across_in(2, last).wait_recv()
    for h, acc in enumerate(blend(last, accs)):
        dense_o[h] = acc / dense_o[h]

    def back(s):
        return pltpu.make_async_remote_copy(
            src_ref=o_send.at[s], dst_ref=o_got.at[u],
            send_sem=osend_sem.at[s], recv_sem=orecv_sem.at[u],
            device_id={"uly": s, "blk": b}, device_id_type=MESH,
        )

    def back_in(s):
        return pltpu.make_async_remote_copy(
            src_ref=o_send.at[s], dst_ref=o_got.at[s],
            send_sem=osend_sem.at[s], recv_sem=orecv_sem.at[s],
            device_id={"uly": s, "blk": b}, device_id_type=MESH,
        )

    def finish(s):
        for i in range(per):
            tile = (s * 2 + b) * per + i
            slot = s * per + i
            rows = jnp.concatenate([V[pat[0, j, tile]] for j in range(listed)], axis=0)
            res = jnp.dot(probs[slot], rows, preferred_element_type=jnp.float32) / total[slot]
            for h in range(heavies):
                res = jnp.where(heavy[0, h] == tile, dense_o[h], res)
            o_send[s, i] = res.astype(jnp.bfloat16)

    def finish_chunk(c, carry):
        s = flip(u, U - 1 - c, U)
        finish(s)
        back(s).start()
        return carry

    lax.fori_loop(0, U - 1, finish_chunk, 0)
    finish(u)

    def place(buf, s):
        for r in range(per):
            wide[r, pl.ds(s, TILE, stride=heads), :] = buf[s, r].astype(jnp.float32)

    place(o_send, u)

    def land(i, c):
        s = flip(u, U - 1 - i, U)
        back_in(s).wait_recv()
        place(o_got, s)
        return c

    lax.fori_loop(0, U - 1, land, 0)
    for r in range(per):
        rows = wide[r].reshape(TILE, heads, head)
        staged[0, r * TILE:(r + 1) * TILE] = rows.astype(jnp.bfloat16)
    written = pltpu.make_async_copy(staged.at[0], out, loc_sem.at[3])
    written.start()

    def close(i, c):
        s = flip(u, i + 1, U)
        for n in range(3):
            if n:
                away(n, s).wait_send()
            across(n, s).wait_send()
        back(s).wait_send()
        return c

    lax.fori_loop(0, U - 1, close, 0)
    for n in range(1, 3):
        own_across(n).wait_send()
    written.wait()


def per_device(queries, keys, values, pattern, heavy):
    tokens, heads, head = queries.shape
    U = lax.axis_size("uly")
    per = tokens // TILE
    tiles = U * 2 * per
    group = 2 * per
    listed, heavies = pattern.shape[2], heavy.shape[1]


    bf = jnp.bfloat16
    any_ = pl.BlockSpec(memory_space=pl.ANY)
    dma = pltpu.SemaphoreType.DMA
    return pl.pallas_call(
        functools.partial(kernel, U, per),
        out_shape=jax.ShapeDtypeStruct((tokens, heads, head), bf),
        in_specs=[any_] * 5,
        out_specs=any_,
        scratch_shapes=[
            pltpu.VMEM((tiles, TILE, head), bf),
            pltpu.VMEM((tiles, TILE, head), bf),
            pltpu.VMEM((tiles, TILE, head), bf),
            pltpu.VMEM((tiles // 2, TILE, listed * TILE), bf),
            pltpu.VMEM((tiles // 2, TILE, head), jnp.float32),
            pltpu.VMEM((heavies, tiles // group, TILE, group * TILE), bf),
            pltpu.VMEM((heavies, TILE, head), jnp.float32),
            pltpu.SMEM((1, listed, tiles), jnp.int32),
            pltpu.SMEM(heavy.shape, jnp.int32),
            pltpu.VMEM((3, tokens, heads, head), bf),
            pltpu.VMEM((per, TILE * heads, head), jnp.float32),
            *[pltpu.VMEM((U, per, TILE, head), bf)] * 4,
            dma((3, U)), dma((3, U)), dma((3, U)), dma((3, U)), dma((4,)), dma((U,)), dma((U,)), dma((5,)),
        ],
        compiler_params=pltpu.CompilerParams(
            collective_id=0, has_side_effects=True, vmem_limit_bytes=60 * 2 ** 20
        ),
    )(pattern.transpose(0, 2, 1), heavy, queries, keys, values)


def solution(mesh):
    rows = P(("grp", "uly", "blk"), None, None)
    placed = (rows, rows, rows, P(("grp", "uly"), None, None), P(("grp", "uly"), None))
    return jax.shard_map(
        per_device, mesh=mesh, in_specs=placed, out_specs=rows, check_vma=False,
    )
```

```python
import functools
import math

import jax
import jax.numpy as jnp
from jax import lax
from jax.experimental import pallas as pl
from jax.experimental.pallas import tpu as pltpu
from jax.sharding import PartitionSpec as P

TILE = 128
MESH = pl.DeviceIdType.MESH


def flip(u, d, count):
    if count & (count - 1):
        return (d + count - u) % count
    out, k = 0, 1
    while k < count:
        out = out + ((u // k + d // k) % 2) * k
        k *= 2
    return out


def kernel(
    U, per, pat_in, heavy_in, q_in, k_in, v_in, out,
    Q, K, V, probs, total, dense_p, dense_o, pat, heavy, staged, wide, k_s, q_s, v_s, o_got,
    send_sem, recv_sem, fsend_sem, frecv_sem, loc_sem, osend_sem, orecv_sem, in_sem,
):
    u, b = lax.axis_index("uly"), lax.axis_index("blk")
    sib = 1 - b
    tiles, head = K.shape[0], K.shape[2]
    listed, heavies = pat.shape[1], heavy.shape[1]
    c2 = head ** (-0.5) * math.log2(math.e)
    group = 2 * per
    bufs, ins = (K, Q, V), (k_s, q_s, v_s)
    heads = staged.shape[2]
    o_send = k_s

    barrier = pltpu.get_barrier_semaphore()

    def greet(d, c):
        pl.semaphore_signal(
            barrier, inc=1, device_id={"uly": flip(u, d, U), "blk": b}, device_id_type=MESH
        )
        return c

    lax.fori_loop(1, U, greet, 0)
    pl.semaphore_signal(barrier, inc=1, device_id={"uly": u, "blk": sib}, device_id_type=MESH)

    def fetch(n):
        return pltpu.make_async_copy((k_in, q_in, v_in)[n], staged.at[n], in_sem.at[n])

    tables = (
        pltpu.make_async_copy(pat_in, pat, in_sem.at[3]),
        pltpu.make_async_copy(heavy_in, heavy, in_sem.at[4]),
    )
    for n in range(3):
        fetch(n).start()
    for copy in tables:
        copy.start()

    def widen(n):
        fetch(n).wait()
        for r in range(per):
            rows = staged[n, r * TILE:(r + 1) * TILE].astype(jnp.float32)
            wide[r] = rows.reshape(TILE * heads, head)

    def split(n, s):
        for r in range(per):
            ins[n][s, r] = wide[r, pl.ds(s, TILE, stride=heads), :].astype(jnp.bfloat16)

    def split_all(s, c):
        split(0, s)
        return c

    widen(0)
    lax.fori_loop(0, U, split_all, 0)
    pl.semaphore_wait(barrier, U)

    def at(buf, s, half):
        return buf.at[pl.ds((s * 2 + half) * per, per)]

    def away(n, s):
        return pltpu.make_async_remote_copy(
            src_ref=ins[n].at[s], dst_ref=at(bufs[n], u, b),
            send_sem=send_sem.at[n, s], recv_sem=recv_sem.at[n, u],
            device_id={"uly": s, "blk": b}, device_id_type=MESH,
        )

    def arriving(n, s):
        return pltpu.make_async_remote_copy(
            src_ref=ins[n].at[s], dst_ref=at(bufs[n], s, b),
            send_sem=send_sem.at[n, s], recv_sem=recv_sem.at[n, s],
            device_id={"uly": s, "blk": b}, device_id_type=MESH,
        )

    def across(n, s):
        return pltpu.make_async_remote_copy(
            src_ref=at(bufs[n], s, b), dst_ref=at(bufs[n], s, b),
            send_sem=fsend_sem.at[n, s], recv_sem=frecv_sem.at[n, s],
            device_id={"uly": u, "blk": sib}, device_id_type=MESH,
        )

    def across_in(n, s):
        return pltpu.make_async_remote_copy(
            src_ref=at(bufs[n], s, sib), dst_ref=at(bufs[n], s, sib),
            send_sem=fsend_sem.at[n, s], recv_sem=frecv_sem.at[n, s],
            device_id={"uly": u, "blk": sib}, device_id_type=MESH,
        )

    def own(n):
        return pltpu.make_async_copy(ins[n].at[u], at(bufs[n], u, b), loc_sem.at[n])

    def own_across(n):
        return pltpu.make_async_remote_copy(
            src_ref=ins[n].at[u], dst_ref=at(bufs[n], u, b),
            send_sem=fsend_sem.at[n, u], recv_sem=frecv_sem.at[n, u],
            device_id={"uly": u, "blk": sib}, device_id_type=MESH,
        )

    def early(s):
        return (s % 2 + s // 2 % 2) % 2 == 0

    def push(i, c, n, first):
        s = flip(u, U - 1 - i, U)

        @pl.when(early(s) == first)
        def _():
            away(n, s).start()

        return c

    def split_one(s, c, n):
        split(n, s)
        return c

    for n in range(3):
        if n:
            widen(n)
            lax.fori_loop(0, U, functools.partial(split_one, n=n), 0)
        lax.fori_loop(0, U - 1, functools.partial(push, n=n, first=True), 0)
        own(n).start()
        own_across(n).start()
    for n in range(3):
        lax.fori_loop(0, U - 1, functools.partial(push, n=n, first=False), 0)

    def relay(n, s):
        arriving(n, s).wait_recv()
        across(n, s).start()

    def pass_on(i, c):
        relay(0, flip(u, U - 1 - i, U))
        return c

    lax.fori_loop(0, U - 1, pass_on, 0)
    own(0).wait()
    own(1).wait()
    for copy in tables:
        copy.wait()

    def take(s, c, n=0):
        across_in(n, s).wait_recv()
        return c

    lax.fori_loop(0, U, take, 0)

    def scores(query, key_rows):
        return lax.dot_general(
            query, key_rows, (((1,), (1,)), ((), ())), preferred_element_type=jnp.float32
        )

    def score_tile(s, i):
        tile = (s * 2 + b) * per + i
        slot = s * per + i
        rows = jnp.concatenate([K[pat[0, j, tile]] for j in range(listed)], axis=0)
        sc = scores(Q[tile], rows)
        top = jnp.max(fold(jnp.maximum, sc), axis=-1, keepdims=True)
        w = jnp.exp2((sc - top) * c2)
        total[slot] = jnp.broadcast_to(jnp.sum(fold(jnp.add, w), axis=-1, keepdims=True), (TILE, head))
        probs[slot] = w.astype(jnp.bfloat16)

    def score_chunk(c, carry):
        s = flip(u, U - 1 - c, U)
        for i in range(per):
            score_tile(s, i)

        return carry

    def relay_and_score(c, carry):
        relay(1, flip(u, U - 1 - c, U))
        return score_chunk(c, carry)

    def fold(op, x):
        parts = [x[:, k * head:(k + 1) * head] for k in range(x.shape[1] // head)]
        while len(parts) > 1:
            parts = [op(*parts[k:k + 2]) if k + 1 < len(parts) else parts[k]
                     for k in range(0, len(parts), 2)]
        return parts[0]

    def dense_scores():
        steps = tiles // group
        asked = [Q[heavy[0, h]] for h in range(heavies)]

        def keys_of(g):
            return K[pl.ds(g * group, group)].reshape(group * TILE, head)

        def top_of(g, tops):
            rows = keys_of(g)
            return tuple(
                jnp.maximum(top, fold(jnp.maximum, scores(query, rows)))
                for query, top in zip(asked, tops)
            )

        tops = lax.fori_loop(
            0, steps, top_of, (jnp.full((TILE, head), -jnp.inf, jnp.float32),) * heavies,
            unroll=math.gcd(steps, 4),
        )
        tops = [jnp.max(top, axis=-1, keepdims=True) for top in tops]

        def weigh(g, accs):
            rows, new = keys_of(g), []
            for h in range(heavies):
                w = jnp.exp2((scores(asked[h], rows) - tops[h]) * c2)
                dense_p[h, g] = w.astype(jnp.bfloat16)
                new.append(accs[h] + fold(jnp.add, w))
            return tuple(new)

        accs = lax.fori_loop(
            0, steps, weigh, (jnp.zeros((TILE, head), jnp.float32),) * heavies,
            unroll=math.gcd(steps, 4),
        )
        for h in range(heavies):
            dense_o[h] = jnp.broadcast_to(
                jnp.sum(accs[h], axis=-1, keepdims=True), (TILE, head)
            )

    def sent_keys(i, c):
        s = flip(u, i + 1, U)
        away(0, s).wait_send()
        return c

    lax.fori_loop(0, U - 1, sent_keys, 0)
    own_across(0).wait_send()
    score_chunk(U - 1, 0)
    lax.fori_loop(0, U - 1, relay_and_score, 0)
    lax.fori_loop(0, U, functools.partial(take, n=1), 0)
    dense_scores()
    own(2).wait()

    def blend(s, accs):
        rows = V[pl.ds(s * 2 * per, 2 * per)].reshape(2 * per * TILE, head)
        return tuple(
            acc + jnp.dot(dense_p[h, s], rows, preferred_element_type=jnp.float32)
            for h, acc in enumerate(accs)
        )

    def relay_and_blend(c, accs):
        s = flip(u, U - 1 - c, U)
        relay(2, s)
        before = jnp.where(c == 0, u, flip(u, U - c, U))
        across_in(2, before).wait_recv()
        return blend(before, accs)

    accs = tuple(jnp.zeros((TILE, head), jnp.float32) for _ in range(heavies))
    accs = lax.fori_loop(0, U - 1, relay_and_blend, accs)
    last = flip(u, 1, U)
    across_in(2, last).wait_recv()
    for h, acc in enumerate(blend(last, accs)):
        dense_o[h] = acc / dense_o[h]

    def back(s):
        return pltpu.make_async_remote_copy(
            src_ref=o_send.at[s], dst_ref=o_got.at[u],
            send_sem=osend_sem.at[s], recv_sem=orecv_sem.at[u],
            device_id={"uly": s, "blk": b}, device_id_type=MESH,
        )

    def back_in(s):
        return pltpu.make_async_remote_copy(
            src_ref=o_send.at[s], dst_ref=o_got.at[s],
            send_sem=osend_sem.at[s], recv_sem=orecv_sem.at[s],
            device_id={"uly": s, "blk": b}, device_id_type=MESH,
        )

    def finish(s):
        for i in range(per):
            tile = (s * 2 + b) * per + i
            slot = s * per + i
            rows = jnp.concatenate([V[pat[0, j, tile]] for j in range(listed)], axis=0)
            res = jnp.dot(probs[slot], rows, preferred_element_type=jnp.float32) / total[slot]
            for h in range(heavies):
                res = jnp.where(heavy[0, h] == tile, dense_o[h], res)
            o_send[s, i] = res.astype(jnp.bfloat16)

    def finish_chunk(c, carry):
        s = flip(u, U - 1 - c, U)
        finish(s)
        back(s).start()
        return carry

    def sent_rows(i, c):
        away(2, flip(u, i + 1, U)).wait_send()
        return c

    lax.fori_loop(0, U - 1, sent_rows, 0)
    lax.fori_loop(0, U - 1, finish_chunk, 0)
    finish(u)

    def place(buf, s):
        for r in range(per):
            wide[r, pl.ds(s, TILE, stride=heads), :] = buf[s, r].astype(jnp.float32)

    place(o_send, u)

    def land(i, c, first):
        s = flip(u, U - 1 - i, U)

        @pl.when(early(s) == first)
        def _():
            back_in(s).wait_recv()
            place(o_got, s)

        return c

    for first in (True, False):
        lax.fori_loop(0, U - 1, functools.partial(land, first=first), 0)
    for r in range(per):
        rows = wide[r].reshape(TILE, heads, head)
        staged[0, r * TILE:(r + 1) * TILE] = rows.astype(jnp.bfloat16)
    written = pltpu.make_async_copy(staged.at[0], out, loc_sem.at[3])
    written.start()

    def close(i, c):
        s = flip(u, i + 1, U)
        for n in range(3):
            if n == 1:
                away(n, s).wait_send()
            across(n, s).wait_send()
        back(s).wait_send()
        return c

    lax.fori_loop(0, U - 1, close, 0)
    for n in range(1, 3):
        own_across(n).wait_send()
    written.wait()


def per_device(queries, keys, values, pattern, heavy):
    tokens, heads, head = queries.shape
    U = lax.axis_size("uly")
    per = tokens // TILE
    tiles = U * 2 * per
    group = 2 * per
    listed, heavies = pattern.shape[2], heavy.shape[1]


    bf = jnp.bfloat16
    any_ = pl.BlockSpec(memory_space=pl.ANY)
    dma = pltpu.SemaphoreType.DMA
    return pl.pallas_call(
        functools.partial(kernel, U, per),
        out_shape=jax.ShapeDtypeStruct((tokens, heads, head), bf),
        in_specs=[any_] * 5,
        out_specs=any_,
        scratch_shapes=[
            pltpu.VMEM((tiles, TILE, head), bf),
            pltpu.VMEM((tiles, TILE, head), bf),
            pltpu.VMEM((tiles, TILE, head), bf),
            pltpu.VMEM((tiles // 2, TILE, listed * TILE), bf),
            pltpu.VMEM((tiles // 2, TILE, head), jnp.float32),
            pltpu.VMEM((heavies, tiles // group, TILE, group * TILE), bf),
            pltpu.VMEM((heavies, TILE, head), jnp.float32),
            pltpu.SMEM((1, listed, tiles), jnp.int32),
            pltpu.SMEM(heavy.shape, jnp.int32),
            pltpu.VMEM((3, tokens, heads, head), bf),
            pltpu.VMEM((per, TILE * heads, head), jnp.float32),
            *[pltpu.VMEM((U, per, TILE, head), bf)] * 4,
            dma((3, U)), dma((3, U)), dma((3, U)), dma((3, U)), dma((4,)), dma((U,)), dma((U,)), dma((5,)),
        ],
        compiler_params=pltpu.CompilerParams(
            collective_id=0, has_side_effects=True, vmem_limit_bytes=60 * 2 ** 20
        ),
    )(pattern.transpose(0, 2, 1), heavy, queries, keys, values)


def solution(mesh):
    rows = P(("grp", "uly", "blk"), None, None)
    placed = (rows, rows, rows, P(("grp", "uly"), None, None), P(("grp", "uly"), None))
    return jax.shard_map(
        per_device, mesh=mesh, in_specs=placed, out_specs=rows, check_vma=False,
    )
```

```python
import functools
import math

import jax
import jax.numpy as jnp
from jax import lax
from jax.experimental import pallas as pl
from jax.experimental.pallas import tpu as pltpu
from jax.sharding import PartitionSpec as P

TILE = 128
MESH = pl.DeviceIdType.MESH


def flip(u, d, count):
    if count & (count - 1):
        return (d + count - u) % count
    out, k = 0, 1
    while k < count:
        out = out + ((u // k + d // k) % 2) * k
        k *= 2
    return out


def kernel(
    U, per, pat_in, heavy_in, q_in, k_in, v_in, out,
    Q, K, V, probs, total, dense_p, dense_o, pat, heavy, staged, wide, k_s, q_s, v_s, o_got,
    send_sem, recv_sem, fsend_sem, frecv_sem, loc_sem, osend_sem, orecv_sem, in_sem,
):
    u, b = lax.axis_index("uly"), lax.axis_index("blk")
    sib = 1 - b
    tiles, head = K.shape[0], K.shape[2]
    listed, heavies = pat.shape[1], heavy.shape[1]
    c2 = head ** (-0.5) * math.log2(math.e)
    group = 2 * per
    bufs, ins = (K, Q, V), (k_s, q_s, v_s)
    heads = staged.shape[2]
    o_send = k_s

    barrier = pltpu.get_barrier_semaphore()

    def greet(d, c):
        pl.semaphore_signal(
            barrier, inc=1, device_id={"uly": flip(u, d, U), "blk": b}, device_id_type=MESH
        )
        return c

    lax.fori_loop(1, U, greet, 0)
    pl.semaphore_signal(barrier, inc=1, device_id={"uly": u, "blk": sib}, device_id_type=MESH)

    def fetch(n):
        return pltpu.make_async_copy((k_in, q_in, v_in)[n], staged.at[n], in_sem.at[n])

    tables = (
        pltpu.make_async_copy(pat_in, pat, in_sem.at[3]),
        pltpu.make_async_copy(heavy_in, heavy, in_sem.at[4]),
    )
    for n in range(3):
        fetch(n).start()
    for copy in tables:
        copy.start()

    def widen(n):
        fetch(n).wait()
        for r in range(per):
            rows = staged[n, r * TILE:(r + 1) * TILE].astype(jnp.float32)
            wide[r] = rows.reshape(TILE * heads, head)

    def split(n, s):
        for r in range(per):
            ins[n][s, r] = wide[r, pl.ds(s, TILE, stride=heads), :].astype(jnp.bfloat16)

    def split_all(s, c):
        split(0, s)
        return c

    widen(0)
    lax.fori_loop(0, U, split_all, 0)
    pl.semaphore_wait(barrier, U)

    def at(buf, s, half):
        return buf.at[pl.ds((s * 2 + half) * per, per)]

    def away(n, s):
        return pltpu.make_async_remote_copy(
            src_ref=ins[n].at[s], dst_ref=at(bufs[n], u, b),
            send_sem=send_sem.at[n, s], recv_sem=recv_sem.at[n, u],
            device_id={"uly": s, "blk": b}, device_id_type=MESH,
        )

    def arriving(n, s):
        return pltpu.make_async_remote_copy(
            src_ref=ins[n].at[s], dst_ref=at(bufs[n], s, b),
            send_sem=send_sem.at[n, s], recv_sem=recv_sem.at[n, s],
            device_id={"uly": s, "blk": b}, device_id_type=MESH,
        )

    def across(n, s):
        return pltpu.make_async_remote_copy(
            src_ref=at(bufs[n], s, b), dst_ref=at(bufs[n], s, b),
            send_sem=fsend_sem.at[n, s], recv_sem=frecv_sem.at[n, s],
            device_id={"uly": u, "blk": sib}, device_id_type=MESH,
        )

    def across_in(n, s):
        return pltpu.make_async_remote_copy(
            src_ref=at(bufs[n], s, sib), dst_ref=at(bufs[n], s, sib),
            send_sem=fsend_sem.at[n, s], recv_sem=frecv_sem.at[n, s],
            device_id={"uly": u, "blk": sib}, device_id_type=MESH,
        )

    def own(n):
        return pltpu.make_async_copy(ins[n].at[u], at(bufs[n], u, b), loc_sem.at[n])

    def own_across(n):
        return pltpu.make_async_remote_copy(
            src_ref=ins[n].at[u], dst_ref=at(bufs[n], u, b),
            send_sem=fsend_sem.at[n, u], recv_sem=frecv_sem.at[n, u],
            device_id={"uly": u, "blk": sib}, device_id_type=MESH,
        )

    for n in range(3):
        def push(i, c, n=n):
            s = flip(u, U - 1 - i, U)
            if n:
                split(n, s)
            away(n, s).start()
            return c

        if n:
            widen(n)
        lax.fori_loop(0, U - 1, push, 0)
        if n:
            split(n, u)
        own(n).start()
        own_across(n).start()

    def relay(n, s):
        arriving(n, s).wait_recv()
        across(n, s).start()

    def pass_on(i, c):
        relay(0, flip(u, U - 1 - i, U))
        return c

    lax.fori_loop(0, U - 1, pass_on, 0)
    own(0).wait()
    own(1).wait()
    for copy in tables:
        copy.wait()

    def take(s, c, n=0):
        across_in(n, s).wait_recv()
        return c

    lax.fori_loop(0, U, take, 0)

    def scores(query, key_rows):
        return lax.dot_general(
            query, key_rows, (((1,), (1,)), ((), ())), preferred_element_type=jnp.float32
        )

    def score_tile(s, i):
        tile = (s * 2 + b) * per + i
        slot = s * per + i
        rows = jnp.concatenate([K[pat[0, j, tile]] for j in range(listed)], axis=0)
        sc = scores(Q[tile], rows)
        top = jnp.max(fold(jnp.maximum, sc), axis=-1, keepdims=True)
        w = jnp.exp2((sc - top) * c2)
        total[slot] = jnp.broadcast_to(jnp.sum(fold(jnp.add, w), axis=-1, keepdims=True), (TILE, head))
        probs[slot] = w.astype(jnp.bfloat16)

    def score_chunk(c, carry):
        s = flip(u, U - 1 - c, U)
        for i in range(per):
            score_tile(s, i)

        return carry

    def relay_and_score(c, carry):
        relay(1, flip(u, U - 1 - c, U))
        return score_chunk(c, carry)

    def fold(op, x):
        parts = [x[:, k * head:(k + 1) * head] for k in range(x.shape[1] // head)]
        while len(parts) > 1:
            parts = [op(*parts[k:k + 2]) if k + 1 < len(parts) else parts[k]
                     for k in range(0, len(parts), 2)]
        return parts[0]

    def dense_scores():
        steps = tiles // group
        asked = [Q[heavy[0, h]] for h in range(heavies)]

        def keys_of(g):
            return K[pl.ds(g * group, group)].reshape(group * TILE, head)

        def top_of(g, tops):
            rows = keys_of(g)
            return tuple(
                jnp.maximum(top, fold(jnp.maximum, scores(query, rows)))
                for query, top in zip(asked, tops)
            )

        tops = lax.fori_loop(
            0, steps, top_of, (jnp.full((TILE, head), -jnp.inf, jnp.float32),) * heavies,
            unroll=math.gcd(steps, 4),
        )
        tops = [jnp.max(top, axis=-1, keepdims=True) for top in tops]

        def weigh(g, accs):
            rows, new = keys_of(g), []
            for h in range(heavies):
                w = jnp.exp2((scores(asked[h], rows) - tops[h]) * c2)
                dense_p[h, g] = w.astype(jnp.bfloat16)
                new.append(accs[h] + fold(jnp.add, w))
            return tuple(new)

        accs = lax.fori_loop(
            0, steps, weigh, (jnp.zeros((TILE, head), jnp.float32),) * heavies,
            unroll=math.gcd(steps, 4),
        )
        for h in range(heavies):
            dense_o[h] = jnp.broadcast_to(
                jnp.sum(accs[h], axis=-1, keepdims=True), (TILE, head)
            )

    def sent_keys(i, c):
        s = flip(u, i + 1, U)
        away(0, s).wait_send()
        return c

    lax.fori_loop(0, U - 1, sent_keys, 0)
    own_across(0).wait_send()
    score_chunk(U - 1, 0)
    lax.fori_loop(0, U - 1, relay_and_score, 0)
    lax.fori_loop(0, U, functools.partial(take, n=1), 0)
    dense_scores()
    own(2).wait()

    def blend(s, accs):
        rows = V[pl.ds(s * 2 * per, 2 * per)].reshape(2 * per * TILE, head)
        return tuple(
            acc + jnp.dot(dense_p[h, s], rows, preferred_element_type=jnp.float32)
            for h, acc in enumerate(accs)
        )

    def relay_and_blend(c, accs):
        s = flip(u, U - 1 - c, U)
        relay(2, s)
        before = jnp.where(c == 0, u, flip(u, U - c, U))
        across_in(2, before).wait_recv()
        return blend(before, accs)

    accs = tuple(jnp.zeros((TILE, head), jnp.float32) for _ in range(heavies))
    accs = lax.fori_loop(0, U - 1, relay_and_blend, accs)
    last = flip(u, 1, U)
    across_in(2, last).wait_recv()
    for h, acc in enumerate(blend(last, accs)):
        dense_o[h] = acc / dense_o[h]

    def back(s):
        return pltpu.make_async_remote_copy(
            src_ref=o_send.at[s], dst_ref=o_got.at[u],
            send_sem=osend_sem.at[s], recv_sem=orecv_sem.at[u],
            device_id={"uly": s, "blk": b}, device_id_type=MESH,
        )

    def back_in(s):
        return pltpu.make_async_remote_copy(
            src_ref=o_send.at[s], dst_ref=o_got.at[s],
            send_sem=osend_sem.at[s], recv_sem=orecv_sem.at[s],
            device_id={"uly": s, "blk": b}, device_id_type=MESH,
        )

    def finish(s):
        for i in range(per):
            tile = (s * 2 + b) * per + i
            slot = s * per + i
            rows = jnp.concatenate([V[pat[0, j, tile]] for j in range(listed)], axis=0)
            res = jnp.dot(probs[slot], rows, preferred_element_type=jnp.float32) / total[slot]
            for h in range(heavies):
                res = jnp.where(heavy[0, h] == tile, dense_o[h], res)
            o_send[s, i] = res.astype(jnp.bfloat16)

    def finish_chunk(c, carry):
        s = flip(u, U - 1 - c, U)
        finish(s)
        back(s).start()
        return carry

    lax.fori_loop(0, U - 1, finish_chunk, 0)
    finish(u)

    def place(buf, s):
        for r in range(per):
            wide[r, pl.ds(s, TILE, stride=heads), :] = buf[s, r].astype(jnp.float32)

    place(o_send, u)

    def land(i, c):
        s = flip(u, U - 1 - i, U)
        back_in(s).wait_recv()
        place(o_got, s)
        return c

    lax.fori_loop(0, U - 1, land, 0)
    for r in range(per):
        rows = wide[r].reshape(TILE, heads, head)
        staged[0, r * TILE:(r + 1) * TILE] = rows.astype(jnp.bfloat16)
    written = pltpu.make_async_copy(staged.at[0], out, loc_sem.at[3])
    written.start()

    def close(i, c):
        s = flip(u, i + 1, U)
        for n in range(3):
            if n:
                away(n, s).wait_send()
            across(n, s).wait_send()
        back(s).wait_send()
        return c

    lax.fori_loop(0, U - 1, close, 0)
    for n in range(1, 3):
        own_across(n).wait_send()
    written.wait()


def per_device(queries, keys, values, pattern, heavy):
    tokens, heads, head = queries.shape
    U = lax.axis_size("uly")
    per = tokens // TILE
    tiles = U * 2 * per
    group = 2 * per
    listed, heavies = pattern.shape[2], heavy.shape[1]


    bf = jnp.bfloat16
    any_ = pl.BlockSpec(memory_space=pl.ANY)
    dma = pltpu.SemaphoreType.DMA
    return pl.pallas_call(
        functools.partial(kernel, U, per),
        out_shape=jax.ShapeDtypeStruct((tokens, heads, head), bf),
        in_specs=[any_] * 5,
        out_specs=any_,
        scratch_shapes=[
            pltpu.VMEM((tiles, TILE, head), bf),
            pltpu.VMEM((tiles, TILE, head), bf),
            pltpu.VMEM((tiles, TILE, head), bf),
            pltpu.VMEM((tiles // 2, TILE, listed * TILE), bf),
            pltpu.VMEM((tiles // 2, TILE, head), jnp.float32),
            pltpu.VMEM((heavies, tiles // group, TILE, group * TILE), bf),
            pltpu.VMEM((heavies, TILE, head), jnp.float32),
            pltpu.SMEM((1, listed, tiles), jnp.int32),
            pltpu.SMEM(heavy.shape, jnp.int32),
            pltpu.VMEM((3, tokens, heads, head), bf),
            pltpu.VMEM((per, TILE * heads, head), jnp.float32),
            *[pltpu.VMEM((U, per, TILE, head), bf)] * 4,
            dma((3, U)), dma((3, U)), dma((3, U)), dma((3, U)), dma((4,)), dma((U,)), dma((U,)), dma((5,)),
        ],
        compiler_params=pltpu.CompilerParams(
            collective_id=0, has_side_effects=True, vmem_limit_bytes=min(60 * 2 ** 20, (tiles * 15 // 32 + 9) * 2 ** 20)
        ),
    )(pattern.transpose(0, 2, 1), heavy, queries, keys, values)


def solution(mesh):
    rows = P(("grp", "uly", "blk"), None, None)
    placed = (rows, rows, rows, P(("grp", "uly"), None, None), P(("grp", "uly"), None))
    return jax.shard_map(
        per_device, mesh=mesh, in_specs=placed, out_specs=rows, check_vma=False,
    )
```
